32 devices in a mesh: row: 4 (over y, core), col: 8 (over z, x).
Axes of the slice: x: 2, y: 2, z: 4, core: 2. Of those that a mesh axis runs over, the one named last changes fastest.
Arguments:
- leaf_rhs: bfloat16 [4, 64, 2048], P('row', 'col'), may hold values from -6 to 6
- leaf_inverse: bfloat16 [4, 2048, 2048], P('row'), may hold values from -0.125 to 0.125
- interpolation: bfloat16 [4, 128, 2048], P('row'), may hold values from -0.5 to 0.5
- ranks: int32 [4], P('row'), may hold values from 32 to 128, as said below
- skeleton_rows: int32 [4, 128], P('row'), may hold values from 0 to 2047, as said below
- root_rows: int32 [4, 128], replicated, may hold values from 0 to 16383, as said below
- root_rhs: float32 [64, 16384], P('col', 'row'), may hold values from -6 to 6
- root_factor: bfloat16 [16384, 4, 4096], P('row', None, 'col')
Outputs:
- leaf_solution: float32 [4, 64, 2048], P('row', 'col')
- root_solution: float32 [64, 16384], P('col', 'row')
The draws below stay inside these ranges and needn't reach their ends.
Inputs may be any that keep to these rules, and one draw needn't show every extreme that they name: `ranks`: some leaf has rank 128. `skeleton_rows`: distinct within each leaf. `root_rows`: all distinct over all leaves and slots.
All inputs are finite; a program needn't handle non-finite values.
Results may differ from the reference program's by a relative error of at most 0.014.
Values may be sent and summed in bfloat16 or wider, within the bound.
A program may use at most 128 MiB of HBM per device.

```python
import math
import jax
import jax.numpy as jnp
from jax import lax

LEAF = 2048
KMAX = 128
RT = 16384
LEAVES = 4
NRHS = 64
SECTIONS = 4
SECTION = 4096
N_ROW = 4


def draw_ranks(key, part):
    drawn = jax.random.randint(key, (LEAVES,), KMAX // 4, KMAX + 1)
    fullest = jax.random.randint(jax.random.fold_in(key, 7), (), 0, LEAVES)
    return drawn.at[fullest].set(KMAX).astype(jnp.int32)


def draw_skeleton_rows(key, part):
    leaf_keys = jax.random.split(key, LEAVES)
    chosen = jax.vmap(lambda one_key: jax.random.permutation(one_key, LEAF)[:KMAX])(leaf_keys)
    return chosen.astype(jnp.int32)


def draw_root_rows(key, part):
    order = jax.random.permutation(key, RT)[:LEAVES * KMAX]
    return order.reshape(LEAVES, KMAX).astype(jnp.int32)


def draw_root_factor(key, part):
    shape = (RT, SECTIONS, SECTION)
    noise = jax.random.normal(key, shape, jnp.float32)
    row_ids = lax.broadcasted_iota(jnp.int32, (RT, 1, 1), 0)
    block_ids = lax.broadcasted_iota(jnp.int32, (1, SECTIONS, 1), 1)
    column_ids = lax.broadcasted_iota(jnp.int32, (1, 1, SECTION), 2)
    block_gap = jnp.abs(block_ids - row_ids // SECTION)
    near_scale = 0.7 / math.sqrt(SECTION)
    far_scale = 1.0 / math.sqrt(RT)
    noise = noise * jnp.where(block_gap == 1, near_scale, far_scale)
    on_diagonal = (block_gap == 0) & (column_ids == row_ids % SECTION)
    return jnp.where(on_diagonal, noise + 1.0, noise).astype(jnp.bfloat16)


def levels(key, dims, cuts, least, top_value):
    level, own = 1.0, jax.random.fold_in(key, 6)
    for dim, parts in cuts:
        steps = jnp.exp(jax.random.uniform(jax.random.fold_in(own, dim), (parts,), jnp.float32, least / len(cuts), top_value / len(cuts)))
        level = level * jnp.repeat(steps, dims[dim] // parts).reshape([-1 if axis == dim else 1 for axis in range(len(dims))])
    return level


def centred(key, dims, scale, reach, cuts=(), kind=jnp.bfloat16):
    array = scale * jax.random.normal(key, dims, jnp.float32)
    if cuts:
        array = array * levels(key, dims, cuts, -0.22, 0.18)
    return jnp.clip(array, -reach, reach).astype(kind)


def setup_inputs(seed: int = 0) -> dict:
    splits = jax.random.split(jax.random.key(seed), 9)
    leaf_rhs = centred(splits[0], (LEAVES, NRHS, LEAF), 1.0, 6.0, ((0, 4), (1, 8)))
    leaf_inverse = centred(splits[1], (LEAVES, LEAF, LEAF), LEAF ** -0.5, 0.125, ((0, 4),))
    interpolation = centred(splits[2], (LEAVES, KMAX, LEAF), KMAX ** -0.5, 0.5, ((0, 4),))
    ranks = draw_ranks(jax.random.fold_in(splits[8], 71), 0)
    skeleton_rows = draw_skeleton_rows(jax.random.fold_in(splits[8], 71), 0)
    root_rows = draw_root_rows(jax.random.fold_in(splits[8], 71), 0)
    root_rhs = centred(splits[6], (NRHS, RT), 1.0, 6.0, ((0, 8), (1, 4)), jnp.float32)
    root_factor = draw_root_factor(jax.random.fold_in(splits[8], 71), 0)
    return {"leaf_rhs": leaf_rhs, "leaf_inverse": leaf_inverse, "interpolation": interpolation, "ranks": ranks, "skeleton_rows": skeleton_rows, "root_rows": root_rows, "root_rhs": root_rhs, "root_factor": root_factor}


def reference(leaf_rhs, leaf_inverse, interpolation, ranks, skeleton_rows, root_rows, root_rhs, root_factor):
    solved = jnp.einsum("lrk,ljk->lrj", leaf_rhs.astype(jnp.float32), leaf_inverse.astype(jnp.float32))
    live_slots = jnp.arange(KMAX, dtype=jnp.int32)[None, :] < ranks[:, None]
    index_table = jnp.broadcast_to(skeleton_rows[:, None, :], (LEAVES, NRHS, KMAX))
    skeleton = jnp.where(live_slots[:, None, :], jnp.take_along_axis(solved, index_table, axis=2), 0.0)
    flat_values = jnp.transpose(skeleton, (1, 0, 2)).reshape(NRHS, LEAVES * KMAX)
    assembled = root_rhs.at[:, root_rows.reshape(-1)].add(flat_values)
    forward_full = []
    forward_low = []
    for block_row in range(N_ROW):
        running = assembled[:, block_row * SECTION:(block_row + 1) * SECTION]
        for block_col in range(block_row):
            factor_block = root_factor[block_row * SECTION:(block_row + 1) * SECTION, block_col, :]
            running = running - jnp.dot(forward_low[block_col], factor_block.T, preferred_element_type=jnp.float32)
        forward_full.append(running)
        forward_low.append(running.astype(jnp.bfloat16))
    solution_full = [None] * N_ROW
    solution_low = [None] * N_ROW
    for block_row in reversed(range(N_ROW)):
        running = forward_full[block_row]
        for block_col in range(block_row + 1, N_ROW):
            factor_block = root_factor[block_row * SECTION:(block_row + 1) * SECTION, block_col, :]
            running = running - jnp.dot(solution_low[block_col], factor_block.T, preferred_element_type=jnp.float32)
        diagonal_block = root_factor[block_row * SECTION:(block_row + 1) * SECTION, block_row, :]
        fresh_block = jnp.dot(running.astype(jnp.bfloat16), diagonal_block.T, preferred_element_type=jnp.float32)
        solution_full[block_row] = fresh_block
        solution_low[block_row] = fresh_block.astype(jnp.bfloat16)
    root_solution = jnp.concatenate(solution_full, axis=1)
    taken = jnp.transpose(root_solution[:, root_rows], (1, 0, 2)).astype(jnp.bfloat16)
    skeleton_solution = jnp.where(live_slots[:, None, :], taken, jnp.zeros_like(taken))
    correction = jnp.einsum("lrk,lkj->lrj", skeleton_solution.astype(jnp.float32), interpolation.astype(jnp.float32))
    leaf_solution = solved - correction
    return (leaf_solution, root_solution)
```

```python
import functools

import jax
import jax.numpy as jnp
from jax import lax
from jax.experimental import pallas as pl
from jax.experimental.pallas import tpu as pltpu
from jax.sharding import PartitionSpec as P

BF16 = jnp.bfloat16
F32 = jnp.float32


def dot_nt(left, right):
    return lax.dot_general(left, right, (((1,), (1,)), ((), ())), preferred_element_type=F32)


def dot_nn(left, right):
    return lax.dot_general(left, right, (((1,), (0,)), ((), ())), preferred_element_type=F32)


def hi_lo(value):
    high = value.astype(BF16)
    low = (value - high.astype(F32)).astype(BF16)
    return jnp.concatenate([high, low], axis=0)


def kernel(
    rows, cols,
    ranks, leaf_rhs, leaf_inverse, interpolation, skeleton_rows, root_rows, root_rhs, factor,
    leaf_out, root_out,
    inverse_v, factor_v, hot, solved, skel_box, assem, assem_box, vec_send, vec_box,
    acc, stage, box, kept, full, sol_box, take, take_box,
    inverse_sem, factor_sem, skel_send_sem, skel_sem, assem_send_sem, assem_sem,
    vec_send_sem, vec_sem, rs_send_sem, rs_sem, sol_send_sem, sol_sem, take_send_sem, take_sem,
):
    row = lax.axis_index("row")
    col = lax.axis_index("col")
    rhs_here, section = root_rhs.shape
    width = section // cols
    slots = skeleton_rows.shape[1]
    leaf = leaf_rhs.shape[1]

    load_inverse = pltpu.make_async_copy(leaf_inverse, inverse_v, inverse_sem)
    load_inverse.start()
    load_factor = pltpu.make_async_copy(factor, factor_v, factor_sem)
    load_factor.start()

    barrier = pltpu.get_barrier_semaphore()
    for step in range(1, rows):
        pl.semaphore_signal(barrier, inc=1, device_id={"row": lax.rem(row + step, rows)})
    for step in range(1, cols):
        pl.semaphore_signal(barrier, inc=1, device_id={"col": lax.rem(col + step, cols)})

    def build_hot(part, carry):
        start = part * width
        at = lax.broadcasted_iota(jnp.int32, (width, slots), 0) + (start + row * section)
        for leaf_index in range(rows):
            wanted = root_rows[leaf_index:leaf_index + 1, :]
            hot[pl.ds(pl.multiple_of(start, width), width),
                leaf_index * slots:(leaf_index + 1) * slots] = jnp.where(
                    at == wanted, 1.0, 0.0).astype(BF16)
        return carry

    lax.fori_loop(0, cols, build_hot, 0)

    live = lax.broadcasted_iota(jnp.int32, (rhs_here, slots), 1) < ranks[0]

    load_inverse.wait()
    leaf_step = 256
    here = leaf_rhs[...]
    skeleton = jnp.zeros((2 * rhs_here, slots), F32)
    for start in range(0, leaf, leaf_step):
        part = dot_nt(here, inverse_v[start:start + leaf_step, :])
        solved[:, start:start + leaf_step] = part
        at = lax.broadcasted_iota(jnp.int32, (leaf_step, slots), 0) + start
        pick = jnp.where(at == skeleton_rows[...], 1.0, 0.0).astype(BF16)
        skeleton = skeleton + dot_nn(hi_lo(part), pick)
    skeleton = jnp.where(live, skeleton[:rhs_here] + skeleton[rhs_here:], 0.0)
    skel_box[row] = skeleton

    pl.semaphore_wait(barrier, rows + cols - 2)

    def skel_copy(target, source):
        return pltpu.make_async_remote_copy(
            skel_box.at[row], skel_box.at[source], skel_send_sem.at[target],
            skel_sem.at[source], device_id={"row": target})

    for step in range(1, rows):
        target = lax.rem(row + step, rows)
        pltpu.make_async_remote_copy(
            skel_box.at[row], skel_box.at[row], skel_send_sem.at[target],
            skel_sem.at[row], device_id={"row": target}).start()
    for step in range(1, rows):
        source = lax.rem(row + step, rows)
        skel_copy(source, source).wait_recv()

    split = [hi_lo(skel_box[leaf_index]) for leaf_index in range(rows)]
    flat = jnp.concatenate(split, axis=1)

    def assem_copy(target, slot):
        return pltpu.make_async_remote_copy(
            assem.at[target], assem_box.at[slot], assem_send_sem.at[target],
            assem_sem.at[slot], device_id={"col": target})

    def build_assem(step, carry):
        target = lax.rem(col + step, cols)
        start = pl.multiple_of(target * width, width)
        added = dot_nt(flat, hot[pl.ds(start, width), :])
        assem[target] = root_rhs[:, pl.ds(start, width)] + (added[:rhs_here] + added[rhs_here:])

        @pl.when(step < cols)
        def _():
            assem_copy(target, col).start()

        return carry

    lax.fori_loop(1, cols + 1, build_assem, 0)
    assem_box[col] = assem[col]

    def take_assem(step, carry):
        source = lax.rem(col + step, cols)
        assem_copy(source, source).wait_recv()
        return carry

    lax.fori_loop(1, cols, take_assem, 0)
    for source in range(cols):
        kept[source * rhs_here:(source + 1) * rhs_here, :] = assem_box[source]

    load_factor.wait()

    def vec_copy(kind, target, slot):
        return pltpu.make_async_remote_copy(
            vec_send.at[kind], vec_box.at[kind, slot], vec_send_sem.at[kind, target],
            vec_sem.at[kind, slot], device_id={"row": target})

    def clear():
        def body(part, carry):
            acc[part] = jnp.zeros(acc.shape[1:], F32)
            return carry
        lax.fori_loop(0, cols, body, 0)

    def block(source, part):
        return factor_v[source, pl.ds(pl.multiple_of(part * width, width), width), :]

    def gather_in(kind, source):
        vec_copy(kind, source, source).wait_recv()

        def body(part, carry):
            acc[part] += dot_nt(vec_box[kind, source], block(source, part))
            return carry

        lax.fori_loop(0, cols, body, 0)

    def rs_copy(phase, target, slot):
        return pltpu.make_async_remote_copy(
            stage.at[phase, target], box.at[phase, slot], rs_send_sem.at[phase, target],
            rs_sem.at[phase, slot], device_id={"col": target})

    def reduce_scatter(phase, vector, source, with_acc):
        def send(step, carry):
            target = lax.rem(col + step, cols)
            part = dot_nt(vector(), block(source, target))
            if with_acc:
                part = part + acc[target]
            stage[phase, target] = part.astype(BF16)
            rs_copy(phase, target, col).start()
            return carry

        lax.fori_loop(1, cols, send, 0)
        total = dot_nt(vector(), block(source, col))
        if with_acc:
            total = total + acc[col]
        full[...] = total

        def receive(step, carry):
            origin = lax.rem(col + cols - step, cols)
            rs_copy(phase, origin, origin).wait_recv()
            full[...] += box[phase, origin].astype(F32)
            return carry

        lax.fori_loop(1, cols, receive, 0)

    @pl.when(row > 0)
    def _():
        clear()

        def body(source, carry):
            gather_in(0, source)
            return carry

        lax.fori_loop(0, row - 1, body, 0)
        vec_copy(0, row - 1, row - 1).wait_recv()
        reduce_scatter(0, lambda: vec_box[0, row - 1], row - 1, True)
        kept[...] = kept[...] - full[...]

    vec_send[0] = kept[...].astype(BF16)
    for step in range(1, rows):
        @pl.when(row + step < rows)
        def _():
            vec_copy(0, row + step, row).start()

    @pl.when(row < rows - 1)
    def _():
        clear()

        def body(step, carry):
            gather_in(1, rows - 1 - step)
            return carry

        lax.fori_loop(0, rows - 2 - row, body, 0)
        vec_copy(1, row + 1, row + 1).wait_recv()
        reduce_scatter(1, lambda: vec_box[1, row + 1], row + 1, True)
        kept[...] = kept[...] - full[...]

    vec_send[2] = kept[...].astype(BF16)
    reduce_scatter(2, lambda: vec_send[2], row, False)
    vec_send[1] = full[...].astype(BF16)
    for step in range(1, rows):
        @pl.when(row - step >= 0)
        def _():
            vec_copy(1, row - step, row).start()

    def sol_copy(target, slot):
        return pltpu.make_async_remote_copy(
            full.at[pl.ds(pl.multiple_of(target * rhs_here, rhs_here), rhs_here), :],
            sol_box.at[slot], sol_send_sem.at[target], sol_sem.at[slot],
            device_id={"col": target})

    def send_sol(step, carry):
        sol_copy(lax.rem(col + step, cols), col).start()
        return carry

    lax.fori_loop(1, cols, send_sol, 0)
    sol_box[col] = full[pl.ds(pl.multiple_of(col * rhs_here, rhs_here), rhs_here), :]

    def receive_sol(step, carry):
        origin = lax.rem(col + cols - step, cols)
        sol_copy(origin, origin).wait_recv()
        return carry

    lax.fori_loop(1, cols, receive_sol, 0)
    taken = jnp.zeros((rhs_here, rows * slots), F32)
    for source in range(cols):
        piece = sol_box[source]
        root_out[:, source * width:(source + 1) * width] = piece
        taken = taken + dot_nn(piece.astype(BF16), hot[source * width:(source + 1) * width, :])
    for leaf_index in range(rows):
        take[leaf_index] = taken[:, leaf_index * slots:(leaf_index + 1) * slots]

    def take_copy(target, slot):
        return pltpu.make_async_remote_copy(
            take.at[target], take_box.at[slot], take_send_sem.at[target],
            take_sem.at[slot], device_id={"row": target})

    for step in range(1, rows):
        take_copy(lax.rem(row + step, rows), row).start()
    take_box[row] = take[row]
    for step in range(1, rows):
        source = lax.rem(row + step, rows)
        take_copy(source, source).wait_recv()
    picked = take_box[0]
    for source in range(1, rows):
        picked = picked + take_box[source]
    picked = jnp.where(live, picked, 0.0).astype(BF16)
    leaf_out[...] = solved[...] - dot_nn(picked, interpolation[...])

    for step in range(1, rows):
        target = lax.rem(row + step, rows)
        skel_copy(target, target).wait_send()
        take_copy(target, row).wait_send()

        @pl.when(row + step < rows)
        def _():
            vec_copy(0, row + step, row).wait_send()

        @pl.when(row - step >= 0)
        def _():
            vec_copy(1, row - step, row).wait_send()

    def drain(step, carry):
        target = lax.rem(col + step, cols)
        assem_copy(target, col).wait_send()
        sol_copy(target, col).wait_send()
        rs_copy(2, target, col).wait_send()

        @pl.when(row > 0)
        def _():
            rs_copy(0, target, col).wait_send()

        @pl.when(row < rows - 1)
        def _():
            rs_copy(1, target, col).wait_send()

        return carry

    lax.fori_loop(1, cols, drain, 0)


def on_device(
    rows, cols,
    leaf_rhs, leaf_inverse, interpolation, ranks, skeleton_rows, root_rows, root_rhs, root_factor
):
    _, rhs_here, leaf = leaf_rhs.shape
    slots = skeleton_rows.shape[1]
    section = root_rhs.shape[1]
    width = section // cols
    rhs = rhs_here * cols
    factor = jnp.transpose(root_factor, (1, 0, 2))
    vmem = pl.BlockSpec(memory_space=pltpu.VMEM)
    smem = pl.BlockSpec(memory_space=pltpu.SMEM)
    hbm = pl.BlockSpec(memory_space=pl.ANY)
    dma = pltpu.SemaphoreType.DMA
    leaf_solution, root_solution = pl.pallas_call(
        functools.partial(kernel, rows, cols),
        out_shape=(
            jax.ShapeDtypeStruct((rhs_here, leaf), F32),
            jax.ShapeDtypeStruct((rhs_here, section), F32),
        ),
        in_specs=[smem, vmem, hbm, vmem, vmem, vmem, vmem, hbm],
        out_specs=(vmem, vmem),
        scratch_shapes=[
            pltpu.VMEM((leaf, leaf), BF16),
            pltpu.VMEM((rows, section, width), BF16),
            pltpu.VMEM((section, rows * slots), BF16),
            pltpu.VMEM((rhs_here, leaf), F32),
            pltpu.VMEM((rows, rhs_here, slots), F32),
            pltpu.VMEM((cols, rhs_here, width), F32),
            pltpu.VMEM((cols, rhs_here, width), F32),
            pltpu.VMEM((3, rhs, width), BF16),
            pltpu.VMEM((2, rows, rhs, width), BF16),
            pltpu.VMEM((cols, rhs, width), F32),
            pltpu.VMEM((3, cols, rhs, width), BF16),
            pltpu.VMEM((3, cols, rhs, width), BF16),
            pltpu.VMEM((rhs, width), F32),
            pltpu.VMEM((rhs, width), F32),
            pltpu.VMEM((cols, rhs_here, width), F32),
            pltpu.VMEM((rows, rhs_here, slots), F32),
            pltpu.VMEM((rows, rhs_here, slots), F32),
            dma, dma,
            dma((rows,)), dma((rows,)), dma((cols,)), dma((cols,)),
            dma((2, rows)), dma((2, rows)), dma((3, cols)), dma((3, cols)),
            dma((cols,)), dma((cols,)), dma((rows,)), dma((rows,)),
        ],
        compiler_params=pltpu.CompilerParams(
            collective_id=0, has_side_effects=True, vmem_limit_bytes=56 * 1024 * 1024),
        name="root_solve",
    )(
        ranks, leaf_rhs[0], leaf_inverse[0], interpolation[0], skeleton_rows, root_rows,
        root_rhs, factor,
    )
    return leaf_solution[None], root_solution


def solution(mesh):
    in_specs = (
        P("row", "col", None),
        P("row", None, None),
        P("row", None, None),
        P("row"),
        P("row", None),
        P(),
        P("col", "row"),
        P("row", None, "col"),
    )
    out_specs = (P("row", "col", None), P("col", "row"))
    return jax.shard_map(
        functools.partial(on_device, mesh.shape["row"], mesh.shape["col"]),
        mesh=mesh, in_specs=in_specs, out_specs=out_specs, check_vma=False,
    )
```

```python
import functools

import jax
import jax.numpy as jnp
from jax import lax
from jax.experimental import pallas as pl
from jax.experimental.pallas import tpu as pltpu
from jax.sharding import PartitionSpec as P

BF16 = jnp.bfloat16
F32 = jnp.float32


def dot_nt(left, right):
    return lax.dot_general(left, right, (((1,), (1,)), ((), ())), preferred_element_type=F32)


def dot_nn(left, right):
    return lax.dot_general(left, right, (((1,), (0,)), ((), ())), preferred_element_type=F32)


def hi_lo(value):
    high = value.astype(BF16)
    low = (value - high.astype(F32)).astype(BF16)
    return jnp.concatenate([high, low], axis=0)


GROUPS = 2


def kernel(
    rows, cols,
    ranks, leaf_rhs, leaf_inverse, interpolation, skeleton_rows, root_rows, root_rhs, factor,
    leaf_out, root_out,
    inverse_v, factor_v, hot, solved, skel_box, assem, assem_box, vec_send, vec_box,
    acc, stage, box, kept, full, sol_box, take, take_box,
    inverse_sem, factor_sem, skel_send_sem, skel_sem, assem_send_sem, assem_sem,
    vec_send_sem, vec_sem, rs_send_sem, rs_sem, sol_send_sem, sol_sem, take_send_sem, take_sem,
):
    row = lax.axis_index("row")
    col = lax.axis_index("col")
    rhs_here, section = root_rhs.shape
    width = section // cols
    slots = skeleton_rows.shape[1]
    leaf = leaf_rhs.shape[1]

    load_inverse = pltpu.make_async_copy(leaf_inverse, inverse_v, inverse_sem)
    load_inverse.start()
    load_factor = pltpu.make_async_copy(factor, factor_v, factor_sem)

    barrier = pltpu.get_barrier_semaphore()
    for step in range(1, rows):
        pl.semaphore_signal(barrier, inc=1, device_id={"row": lax.rem(row + step, rows)})
    for step in range(1, cols):
        pl.semaphore_signal(barrier, inc=1, device_id={"col": lax.rem(col + step, cols)})

    def build_hot(part, carry):
        start = part * width
        at = lax.broadcasted_iota(jnp.int32, (width, slots), 0) + (start + row * section)
        for leaf_index in range(rows):
            wanted = root_rows[leaf_index:leaf_index + 1, :]
            hot[pl.ds(pl.multiple_of(start, width), width),
                leaf_index * slots:(leaf_index + 1) * slots] = jnp.where(
                    at == wanted, 1.0, 0.0).astype(BF16)
        return carry

    lax.fori_loop(0, cols, build_hot, 0)

    live = lax.broadcasted_iota(jnp.int32, (rhs_here, slots), 1) < ranks[0]

    load_inverse.wait()
    load_factor.start()
    leaf_step = 256
    here = leaf_rhs[...]
    skeleton = jnp.zeros((2 * rhs_here, slots), F32)
    for start in range(0, leaf, leaf_step):
        part = dot_nt(here, inverse_v[start:start + leaf_step, :])
        solved[:, start:start + leaf_step] = part
        at = lax.broadcasted_iota(jnp.int32, (leaf_step, slots), 0) + start
        pick = jnp.where(at == skeleton_rows[...], 1.0, 0.0).astype(BF16)
        skeleton = skeleton + dot_nn(hi_lo(part), pick)
    skeleton = jnp.where(live, skeleton[:rhs_here] + skeleton[rhs_here:], 0.0)
    skel_box[row] = skeleton

    pl.semaphore_wait(barrier, rows + cols - 2)

    def skel_copy(target, source):
        return pltpu.make_async_remote_copy(
            skel_box.at[row], skel_box.at[source], skel_send_sem.at[target],
            skel_sem.at[source], device_id={"row": target})

    for step in range(1, rows):
        target = lax.rem(row + step, rows)
        pltpu.make_async_remote_copy(
            skel_box.at[row], skel_box.at[row], skel_send_sem.at[target],
            skel_sem.at[row], device_id={"row": target}).start()
    for step in range(1, rows):
        source = lax.rem(row + step, rows)
        skel_copy(source, source).wait_recv()

    split = [hi_lo(skel_box[leaf_index]) for leaf_index in range(rows)]
    flat = jnp.concatenate(split, axis=1)

    def assem_copy(target, slot):
        return pltpu.make_async_remote_copy(
            assem.at[target], assem_box.at[slot], assem_send_sem.at[target],
            assem_sem.at[slot], device_id={"col": target})

    def build_assem(step, carry):
        target = lax.rem(col + step, cols)
        start = pl.multiple_of(target * width, width)
        added = dot_nt(flat, hot[pl.ds(start, width), :])
        assem[target] = root_rhs[:, pl.ds(start, width)] + (added[:rhs_here] + added[rhs_here:])

        @pl.when(step < cols)
        def _():
            assem_copy(target, col).start()

        return carry

    lax.fori_loop(1, cols + 1, build_assem, 0)
    assem_box[col] = assem[col]

    def take_assem(step, carry):
        source = lax.rem(col + step, cols)
        assem_copy(source, source).wait_recv()
        return carry

    lax.fori_loop(1, cols, take_assem, 0)
    for source in range(cols):
        kept[source * rhs_here:(source + 1) * rhs_here, :] = assem_box[source]

    load_factor.wait()

    share = rhs_here * cols // GROUPS

    def part_of(group):
        return pl.ds(group * share, share)

    def vec_copy(kind, group, target, slot):
        return pltpu.make_async_remote_copy(
            vec_send.at[kind, part_of(group)], vec_box.at[kind, slot, part_of(group)],
            vec_send_sem.at[kind, target, group], vec_sem.at[kind, slot, group],
            device_id={"row": target})

    def clear():
        def body(part, carry):
            acc[part] = jnp.zeros(acc.shape[1:], F32)
            return carry
        lax.fori_loop(0, cols, body, 0)

    def block(source, part):
        return factor_v[source, pl.ds(pl.multiple_of(part * width, width), width), :]

    def gather_in(kind, group, source):
        vec_copy(kind, group, source, source).wait_recv()

        def body(part, carry):
            acc[part, part_of(group), :] += dot_nt(
                vec_box[kind, source, part_of(group), :], block(source, part))
            return carry

        lax.fori_loop(0, cols, body, 0, unroll=True)

    def rs_copy(phase, group, target, slot):
        return pltpu.make_async_remote_copy(
            stage.at[phase, target, part_of(group)], box.at[phase, slot, part_of(group)],
            rs_send_sem.at[phase, target, group], rs_sem.at[phase, slot, group],
            device_id={"col": target})

    def scatter(phase, group, vector, source, with_acc):
        def send(step, carry):
            target = lax.rem(col + step, cols)
            part = dot_nt(vector, block(source, target))
            if with_acc:
                part = part + acc[target, part_of(group), :]
            stage[phase, target, part_of(group), :] = part.astype(BF16)
            rs_copy(phase, group, target, col).start()
            return carry

        lax.fori_loop(1, cols, send, 0, unroll=True)
        total = dot_nt(vector, block(source, col))
        if with_acc:
            total = total + acc[col, part_of(group), :]
        full[part_of(group), :] = total

    def collect(phase, group):
        total = full[part_of(group), :]
        for step in range(1, cols):
            origin = lax.rem(col + cols - step, cols)
            rs_copy(phase, group, origin, origin).wait_recv()
            total = total + box[phase, origin, part_of(group), :].astype(F32)
        return total

    def send_forward(group):
        vec_send[0, part_of(group), :] = kept[part_of(group), :].astype(BF16)
        for step in range(1, rows):
            @pl.when(row + step < rows)
            def _():
                vec_copy(0, group, row + step, row).start()

    @pl.when(row == 0)
    def _():
        for group in range(GROUPS):
            send_forward(group)

    @pl.when(row > 0)
    def _():
        clear()

        def body(source, carry):
            for group in range(GROUPS):
                gather_in(0, group, source)
            return carry

        lax.fori_loop(0, row - 1, body, 0)
        for group in range(GROUPS):
            vec_copy(0, group, row - 1, row - 1).wait_recv()
            scatter(0, group, vec_box[0, row - 1, part_of(group), :], row - 1, True)

        @pl.when(row < rows - 1)
        def _():
            for group in range(GROUPS):
                kept[part_of(group), :] -= collect(0, group)
                send_forward(group)

    @pl.when(row < rows - 1)
    def _():
        clear()

        def body(step, carry):
            for group in range(GROUPS):
                gather_in(1, group, rows - 1 - step)
            return carry

        lax.fori_loop(0, rows - 2 - row, body, 0)
        for group in range(GROUPS):
            vec_copy(1, group, row + 1, row + 1).wait_recv()
            scatter(1, group, vec_box[1, row + 1, part_of(group), :], row + 1, True)

    last = jnp.where(row == rows - 1, 0, 1)
    for group in range(GROUPS):
        low = (kept[part_of(group), :] - collect(last, group)).astype(BF16)
        scatter(2, group, low, row, False)
    for group in range(GROUPS):
        total = collect(2, group)
        full[part_of(group), :] = total
        vec_send[1, part_of(group), :] = total.astype(BF16)
        for step in range(1, rows):
            @pl.when(row - step >= 0)
            def _():
                vec_copy(1, group, row - step, row).start()

    def sol_copy(target, slot):
        return pltpu.make_async_remote_copy(
            full.at[pl.ds(pl.multiple_of(target * rhs_here, rhs_here), rhs_here), :],
            sol_box.at[slot], sol_send_sem.at[target], sol_sem.at[slot],
            device_id={"col": target})

    def send_sol(step, carry):
        sol_copy(lax.rem(col + step, cols), col).start()
        return carry

    lax.fori_loop(1, cols, send_sol, 0)
    sol_box[col] = full[pl.ds(pl.multiple_of(col * rhs_here, rhs_here), rhs_here), :]

    def receive_sol(step, carry):
        origin = lax.rem(col + cols - step, cols)
        sol_copy(origin, origin).wait_recv()
        return carry

    lax.fori_loop(1, cols, receive_sol, 0)
    taken = jnp.zeros((rhs_here, rows * slots), F32)
    for source in range(cols):
        piece = sol_box[source]
        root_out[:, source * width:(source + 1) * width] = piece
        taken = taken + dot_nn(piece.astype(BF16), hot[source * width:(source + 1) * width, :])
    for leaf_index in range(rows):
        take[leaf_index] = taken[:, leaf_index * slots:(leaf_index + 1) * slots]

    def take_copy(target, slot):
        return pltpu.make_async_remote_copy(
            take.at[target], take_box.at[slot], take_send_sem.at[target],
            take_sem.at[slot], device_id={"row": target})

    for step in range(1, rows):
        take_copy(lax.rem(row + step, rows), row).start()
    take_box[row] = take[row]
    for step in range(1, rows):
        source = lax.rem(row + step, rows)
        take_copy(source, source).wait_recv()
    picked = take_box[0]
    for source in range(1, rows):
        picked = picked + take_box[source]
    picked = jnp.where(live, picked, 0.0).astype(BF16)
    leaf_out[...] = solved[...] - dot_nn(picked, interpolation[...])

    for step in range(1, rows):
        target = lax.rem(row + step, rows)
        skel_copy(target, target).wait_send()
        take_copy(target, row).wait_send()

        for group in range(GROUPS):
            @pl.when(row + step < rows)
            def _():
                vec_copy(0, group, row + step, row).wait_send()

            @pl.when(row - step >= 0)
            def _():
                vec_copy(1, group, row - step, row).wait_send()

    def drain(step, carry):
        target = lax.rem(col + step, cols)
        assem_copy(target, col).wait_send()
        sol_copy(target, col).wait_send()
        for group in range(GROUPS):
            rs_copy(2, group, target, col).wait_send()

            @pl.when(row > 0)
            def _():
                rs_copy(0, group, target, col).wait_send()

            @pl.when(row < rows - 1)
            def _():
                rs_copy(1, group, target, col).wait_send()

        return carry

    lax.fori_loop(1, cols, drain, 0)


def on_device(
    rows, cols,
    leaf_rhs, leaf_inverse, interpolation, ranks, skeleton_rows, root_rows, root_rhs, root_factor
):
    _, rhs_here, leaf = leaf_rhs.shape
    slots = skeleton_rows.shape[1]
    section = root_rhs.shape[1]
    width = section // cols
    rhs = rhs_here * cols
    factor = jnp.transpose(root_factor, (1, 0, 2))
    vmem = pl.BlockSpec(memory_space=pltpu.VMEM)
    smem = pl.BlockSpec(memory_space=pltpu.SMEM)
    hbm = pl.BlockSpec(memory_space=pl.ANY)
    dma = pltpu.SemaphoreType.DMA
    leaf_solution, root_solution = pl.pallas_call(
        functools.partial(kernel, rows, cols),
        out_shape=(
            jax.ShapeDtypeStruct((rhs_here, leaf), F32),
            jax.ShapeDtypeStruct((rhs_here, section), F32),
        ),
        in_specs=[smem, vmem, hbm, vmem, vmem, vmem, vmem, hbm],
        out_specs=(vmem, vmem),
        scratch_shapes=[
            pltpu.VMEM((leaf, leaf), BF16),
            pltpu.VMEM((rows, section, width), BF16),
            pltpu.VMEM((section, rows * slots), BF16),
            pltpu.VMEM((rhs_here, leaf), F32),
            pltpu.VMEM((rows, rhs_here, slots), F32),
            pltpu.VMEM((cols, rhs_here, width), F32),
            pltpu.VMEM((cols, rhs_here, width), F32),
            pltpu.VMEM((2, rhs, width), BF16),
            pltpu.VMEM((2, rows, rhs, width), BF16),
            pltpu.VMEM((cols, rhs, width), F32),
            pltpu.VMEM((3, cols, rhs, width), BF16),
            pltpu.VMEM((3, cols, rhs, width), BF16),
            pltpu.VMEM((rhs, width), F32),
            pltpu.VMEM((rhs, width), F32),
            pltpu.VMEM((cols, rhs_here, width), F32),
            pltpu.VMEM((rows, rhs_here, slots), F32),
            pltpu.VMEM((rows, rhs_here, slots), F32),
            dma, dma,
            dma((rows,)), dma((rows,)), dma((cols,)), dma((cols,)),
            dma((2, rows, GROUPS)), dma((2, rows, GROUPS)),
            dma((3, cols, GROUPS)), dma((3, cols, GROUPS)),
            dma((cols,)), dma((cols,)), dma((rows,)), dma((rows,)),
        ],
        compiler_params=pltpu.CompilerParams(
            collective_id=0, has_side_effects=True, vmem_limit_bytes=56 * 1024 * 1024),
        name="root_solve",
    )(
        ranks, leaf_rhs[0], leaf_inverse[0], interpolation[0], skeleton_rows, root_rows,
        root_rhs, factor,
    )
    return leaf_solution[None], root_solution


def solution(mesh):
    in_specs = (
        P("row", "col", None),
        P("row", None, None),
        P("row", None, None),
        P("row"),
        P("row", None),
        P(),
        P("col", "row"),
        P("row", None, "col"),
    )
    out_specs = (P("row", "col", None), P("col", "row"))
    return jax.shard_map(
        functools.partial(on_device, mesh.shape["row"], mesh.shape["col"]),
        mesh=mesh, in_specs=in_specs, out_specs=out_specs, check_vma=False,
    )
```

```python
import functools

import jax
import jax.numpy as jnp
from jax import lax
from jax.experimental import pallas as pl
from jax.experimental.pallas import tpu as pltpu
from jax.sharding import PartitionSpec as P

BF16 = jnp.bfloat16
F32 = jnp.float32


def dot_nt(left, right):
    return lax.dot_general(left, right, (((1,), (1,)), ((), ())), preferred_element_type=F32)


def dot_nn(left, right):
    return lax.dot_general(left, right, (((1,), (0,)), ((), ())), preferred_element_type=F32)


def hi_lo(value):
    high = value.astype(BF16)
    low = (value - high.astype(F32)).astype(BF16)
    return jnp.concatenate([high, low], axis=0)


GROUPS = 2


def kernel(
    rows, cols,
    ranks, leaf_rhs, leaf_inverse, interpolation, skeleton_rows, root_rows, root_rhs, factor,
    leaf_out, root_out,
    inverse_v, factor_v, hot, solved, skel_box, assem, assem_box, vec_send, vec_box,
    acc, stage, box, kept, own, full, sol_box, take, take_box,
    inverse_sem, factor_sem, skel_send_sem, skel_sem, assem_send_sem, assem_sem,
    vec_send_sem, vec_sem, rs_send_sem, rs_sem, sol_send_sem, sol_sem, take_send_sem, take_sem,
):
    row = lax.axis_index("row")
    col = lax.axis_index("col")
    rhs_here, section = root_rhs.shape
    width = section // cols
    slots = skeleton_rows.shape[1]
    leaf = leaf_rhs.shape[1]

    load_inverse = pltpu.make_async_copy(leaf_inverse, inverse_v, inverse_sem)
    load_inverse.start()
    load_factor = pltpu.make_async_copy(factor, factor_v, factor_sem)

    barrier = pltpu.get_barrier_semaphore()
    for step in range(1, rows):
        pl.semaphore_signal(barrier, inc=1, device_id={"row": lax.rem(row + step, rows)})
    for step in range(1, cols):
        pl.semaphore_signal(barrier, inc=1, device_id={"col": lax.rem(col + step, cols)})

    def build_hot(part, carry):
        start = part * width
        at = lax.broadcasted_iota(jnp.int32, (width, slots), 0) + (start + row * section)
        for leaf_index in range(rows):
            wanted = root_rows[leaf_index:leaf_index + 1, :]
            hot[pl.ds(pl.multiple_of(start, width), width),
                leaf_index * slots:(leaf_index + 1) * slots] = jnp.where(
                    at == wanted, 1.0, 0.0).astype(BF16)
        return carry

    lax.fori_loop(0, cols, build_hot, 0)

    live = lax.broadcasted_iota(jnp.int32, (rhs_here, slots), 1) < ranks[0]

    load_inverse.wait()
    load_factor.start()
    leaf_step = 256
    here = leaf_rhs[...]
    skeleton = jnp.zeros((2 * rhs_here, slots), F32)
    for start in range(0, leaf, leaf_step):
        part = dot_nt(here, inverse_v[start:start + leaf_step, :])
        solved[:, start:start + leaf_step] = part
        at = lax.broadcasted_iota(jnp.int32, (leaf_step, slots), 0) + start
        pick = jnp.where(at == skeleton_rows[...], 1.0, 0.0).astype(BF16)
        skeleton = skeleton + dot_nn(hi_lo(part), pick)
    skeleton = jnp.where(live, skeleton[:rhs_here] + skeleton[rhs_here:], 0.0)
    skel_box[row] = skeleton

    pl.semaphore_wait(barrier, rows + cols - 2)

    def skel_copy(target, source):
        return pltpu.make_async_remote_copy(
            skel_box.at[row], skel_box.at[source], skel_send_sem.at[target],
            skel_sem.at[source], device_id={"row": target})

    for step in range(1, rows):
        target = lax.rem(row + step, rows)
        pltpu.make_async_remote_copy(
            skel_box.at[row], skel_box.at[row], skel_send_sem.at[target],
            skel_sem.at[row], device_id={"row": target}).start()
    for step in range(1, rows):
        source = lax.rem(row + step, rows)
        skel_copy(source, source).wait_recv()

    split = [hi_lo(skel_box[leaf_index]) for leaf_index in range(rows)]
    flat = jnp.concatenate(split, axis=1)

    def assem_copy(target, slot):
        return pltpu.make_async_remote_copy(
            assem.at[target], assem_box.at[slot], assem_send_sem.at[target],
            assem_sem.at[slot], device_id={"col": target})

    def build_assem(step, carry):
        target = lax.rem(col + step, cols)
        start = pl.multiple_of(target * width, width)
        added = dot_nt(flat, hot[pl.ds(start, width), :])
        assem[target] = root_rhs[:, pl.ds(start, width)] + (added[:rhs_here] + added[rhs_here:])

        @pl.when(step < cols)
        def _():
            assem_copy(target, col).start()

        return carry

    lax.fori_loop(1, cols + 1, build_assem, 0)
    assem_box[col] = assem[col]

    def take_assem(step, carry):
        source = lax.rem(col + step, cols)
        assem_copy(source, source).wait_recv()
        return carry

    lax.fori_loop(1, cols, take_assem, 0)
    share = rhs_here * cols // GROUPS
    lanes = kept.shape[2]
    fold = lanes // share
    tall = width // fold

    def packed(value):
        return jnp.concatenate(
            [value[at * tall:(at + 1) * tall, :] for at in range(fold)], axis=1)

    def unpacked(value):
        return jnp.concatenate(
            [value[:, at * share:(at + 1) * share] for at in range(fold)], axis=0)

    tile = jnp.concatenate([assem_box[source] for source in range(cols)], axis=0)
    if tile.shape[0] < lanes:
        tile = jnp.concatenate(
            [tile, jnp.zeros((lanes - tile.shape[0], width), F32)], axis=0)
    turned = jnp.transpose(tile)
    for group in range(GROUPS):
        kept[group] = packed(turned[:, group * share:(group + 1) * share])

    load_factor.wait()

    def vec_copy(kind, group, target, slot):
        return pltpu.make_async_remote_copy(
            vec_send.at[kind, group], vec_box.at[kind, slot, group],
            vec_send_sem.at[kind, target, group], vec_sem.at[kind, slot, group],
            device_id={"row": target})

    def clear():
        def body(part, carry):
            acc[part] = jnp.zeros(acc.shape[1:], F32)
            return carry
        lax.fori_loop(0, cols, body, 0)

    def block(source, part):
        return factor_v[source, pl.ds(pl.multiple_of(part * width, width), width), :]

    def vector_of(kind, group, source):
        return unpacked(vec_box[kind, source, group].astype(F32)).astype(BF16)

    def gather_in(kind, group, source):
        vec_copy(kind, group, source, source).wait_recv()

        vector = vector_of(kind, group, source)

        def body(part, carry):
            acc[part, group] += packed(dot_nn(block(source, part), vector))
            return carry

        lax.fori_loop(0, cols, body, 0, unroll=True)

    def rs_copy(phase, group, target, slot):
        return pltpu.make_async_remote_copy(
            stage.at[phase, target, group], box.at[phase, slot, group],
            rs_send_sem.at[phase, target, group], rs_sem.at[phase, slot, group],
            device_id={"col": target})

    def scatter(phase, group, vector, source, with_acc):
        def send(step, carry):
            target = lax.rem(col + step, cols)
            part = packed(dot_nn(block(source, target), vector))
            if with_acc:
                part = part + acc[target, group]
            stage[phase, target, group] = part.astype(BF16)
            rs_copy(phase, group, target, col).start()
            return carry

        lax.fori_loop(1, cols, send, 0, unroll=True)
        total = packed(dot_nn(block(source, col), vector))
        if with_acc:
            total = total + acc[col, group]
        own[group] = total

    def collect(phase, group):
        total = own[group]
        for step in range(1, cols):
            origin = lax.rem(col + cols - step, cols)
            rs_copy(phase, group, origin, origin).wait_recv()
            total = total + box[phase, origin, group].astype(F32)
        return total

    def send_forward(group):
        vec_send[0, group] = kept[group].astype(BF16)
        for step in range(1, rows):
            @pl.when(row + step < rows)
            def _():
                vec_copy(0, group, row + step, row).start()

    @pl.when(row == 0)
    def _():
        for group in range(GROUPS):
            send_forward(group)

    @pl.when(row > 0)
    def _():
        clear()

        def body(source, carry):
            for group in range(GROUPS):
                gather_in(0, group, source)
            return carry

        lax.fori_loop(0, row - 1, body, 0)
        for group in range(GROUPS):
            vec_copy(0, group, row - 1, row - 1).wait_recv()
            scatter(0, group, vector_of(0, group, row - 1), row - 1, True)

        @pl.when(row < rows - 1)
        def _():
            for group in range(GROUPS):
                kept[group] -= collect(0, group)
                send_forward(group)

    @pl.when(row < rows - 1)
    def _():
        clear()

        def body(step, carry):
            for group in range(GROUPS):
                gather_in(1, group, rows - 1 - step)
            return carry

        lax.fori_loop(0, rows - 2 - row, body, 0)
        for group in range(GROUPS):
            vec_copy(1, group, row + 1, row + 1).wait_recv()
            scatter(1, group, vector_of(1, group, row + 1), row + 1, True)

    last = jnp.where(row == rows - 1, 0, 1)
    for group in range(GROUPS):
        low = unpacked(kept[group] - collect(last, group)).astype(BF16)
        scatter(2, group, low, row, False)
    for group in range(GROUPS):
        total = collect(2, group)
        own[group] = total
        vec_send[1, group] = total.astype(BF16)
        for step in range(1, rows):
            @pl.when(row - step >= 0)
            def _():
                vec_copy(1, group, row - step, row).start()

    turned = jnp.concatenate([unpacked(own[group]) for group in range(GROUPS)], axis=1)
    if turned.shape[1] < lanes:
        turned = jnp.concatenate(
            [turned, jnp.zeros((width, lanes - turned.shape[1]), F32)], axis=1)
    full[...] = jnp.transpose(turned)[:full.shape[0], :]

    def sol_copy(target, slot):
        return pltpu.make_async_remote_copy(
            full.at[pl.ds(pl.multiple_of(target * rhs_here, rhs_here), rhs_here), :],
            sol_box.at[slot], sol_send_sem.at[target], sol_sem.at[slot],
            device_id={"col": target})

    def send_sol(step, carry):
        sol_copy(lax.rem(col + step, cols), col).start()
        return carry

    lax.fori_loop(1, cols, send_sol, 0)
    sol_box[col] = full[pl.ds(pl.multiple_of(col * rhs_here, rhs_here), rhs_here), :]

    def receive_sol(step, carry):
        origin = lax.rem(col + cols - step, cols)
        sol_copy(origin, origin).wait_recv()
        return carry

    lax.fori_loop(1, cols, receive_sol, 0)
    taken = jnp.zeros((rhs_here, rows * slots), F32)
    for source in range(cols):
        piece = sol_box[source]
        root_out[:, source * width:(source + 1) * width] = piece
        taken = taken + dot_nn(piece.astype(BF16), hot[source * width:(source + 1) * width, :])
    for leaf_index in range(rows):
        take[leaf_index] = taken[:, leaf_index * slots:(leaf_index + 1) * slots]

    def take_copy(target, slot):
        return pltpu.make_async_remote_copy(
            take.at[target], take_box.at[slot], take_send_sem.at[target],
            take_sem.at[slot], device_id={"row": target})

    for step in range(1, rows):
        take_copy(lax.rem(row + step, rows), row).start()
    take_box[row] = take[row]
    for step in range(1, rows):
        source = lax.rem(row + step, rows)
        take_copy(source, source).wait_recv()
    picked = take_box[0]
    for source in range(1, rows):
        picked = picked + take_box[source]
    picked = jnp.where(live, picked, 0.0).astype(BF16)
    leaf_out[...] = solved[...] - dot_nn(picked, interpolation[...])

    for step in range(1, rows):
        target = lax.rem(row + step, rows)
        skel_copy(target, target).wait_send()
        take_copy(target, row).wait_send()

        for group in range(GROUPS):
            @pl.when(row + step < rows)
            def _():
                vec_copy(0, group, row + step, row).wait_send()

            @pl.when(row - step >= 0)
            def _():
                vec_copy(1, group, row - step, row).wait_send()

    def drain(step, carry):
        target = lax.rem(col + step, cols)
        assem_copy(target, col).wait_send()
        sol_copy(target, col).wait_send()
        for group in range(GROUPS):
            rs_copy(2, group, target, col).wait_send()

            @pl.when(row > 0)
            def _():
                rs_copy(0, group, target, col).wait_send()

            @pl.when(row < rows - 1)
            def _():
                rs_copy(1, group, target, col).wait_send()

        return carry

    lax.fori_loop(1, cols, drain, 0)


def on_device(
    rows, cols,
    leaf_rhs, leaf_inverse, interpolation, ranks, skeleton_rows, root_rows, root_rhs, root_factor
):
    _, rhs_here, leaf = leaf_rhs.shape
    slots = skeleton_rows.shape[1]
    section = root_rhs.shape[1]
    width = section // cols
    rhs = rhs_here * cols
    lanes = 128
    folded = (GROUPS, rhs * width // (GROUPS * lanes), lanes)
    factor = jnp.transpose(root_factor, (1, 0, 2))
    vmem = pl.BlockSpec(memory_space=pltpu.VMEM)
    smem = pl.BlockSpec(memory_space=pltpu.SMEM)
    hbm = pl.BlockSpec(memory_space=pl.ANY)
    dma = pltpu.SemaphoreType.DMA
    leaf_solution, root_solution = pl.pallas_call(
        functools.partial(kernel, rows, cols),
        out_shape=(
            jax.ShapeDtypeStruct((rhs_here, leaf), F32),
            jax.ShapeDtypeStruct((rhs_here, section), F32),
        ),
        in_specs=[smem, vmem, hbm, vmem, vmem, vmem, vmem, hbm],
        out_specs=(vmem, vmem),
        scratch_shapes=[
            pltpu.VMEM((leaf, leaf), BF16),
            pltpu.VMEM((rows, section, width), BF16),
            pltpu.VMEM((section, rows * slots), BF16),
            pltpu.VMEM((rhs_here, leaf), F32),
            pltpu.VMEM((rows, rhs_here, slots), F32),
            pltpu.VMEM((cols, rhs_here, width), F32),
            pltpu.VMEM((cols, rhs_here, width), F32),
            pltpu.VMEM((2,) + folded, BF16),
            pltpu.VMEM((2, rows) + folded, BF16),
            pltpu.VMEM((cols,) + folded, F32),
            pltpu.VMEM((3, cols) + folded, BF16),
            pltpu.VMEM((3, cols) + folded, BF16),
            pltpu.VMEM(folded, F32),
            pltpu.VMEM(folded, F32),
            pltpu.VMEM((rhs, width), F32),
            pltpu.VMEM((cols, rhs_here, width), F32),
            pltpu.VMEM((rows, rhs_here, slots), F32),
            pltpu.VMEM((rows, rhs_here, slots), F32),
            dma, dma,
            dma((rows,)), dma((rows,)), dma((cols,)), dma((cols,)),
            dma((2, rows, GROUPS)), dma((2, rows, GROUPS)),
            dma((3, cols, GROUPS)), dma((3, cols, GROUPS)),
            dma((cols,)), dma((cols,)), dma((rows,)), dma((rows,)),
        ],
        compiler_params=pltpu.CompilerParams(
            collective_id=0, has_side_effects=True, vmem_limit_bytes=56 * 1024 * 1024),
        name="root_solve",
    )(
        ranks, leaf_rhs[0], leaf_inverse[0], interpolation[0], skeleton_rows, root_rows,
        root_rhs, factor,
    )
    return leaf_solution[None], root_solution


def solution(mesh):
    in_specs = (
        P("row", "col", None),
        P("row", None, None),
        P("row", None, None),
        P("row"),
        P("row", None),
        P(),
        P("col", "row"),
        P("row", None, "col"),
    )
    out_specs = (P("row", "col", None), P("col", "row"))
    return jax.shard_map(
        functools.partial(on_device, mesh.shape["row"], mesh.shape["col"]),
        mesh=mesh, in_specs=in_specs, out_specs=out_specs, check_vma=False,
    )
```

```python
import functools

import jax
import jax.numpy as jnp
from jax import lax
from jax.experimental import pallas as pl
from jax.experimental.pallas import tpu as pltpu
from jax.sharding import PartitionSpec as P

BF16 = jnp.bfloat16
F32 = jnp.float32


def dot_nt(left, right):
    return lax.dot_general(left, right, (((1,), (1,)), ((), ())), preferred_element_type=F32)


def dot_nn(left, right):
    return lax.dot_general(left, right, (((1,), (0,)), ((), ())), preferred_element_type=F32)


def hi_lo(value):
    high = value.astype(BF16)
    low = (value - high.astype(F32)).astype(BF16)
    return jnp.concatenate([high, low], axis=0)


GROUPS = 1


def kernel(
    rows, cols,
    ranks, leaf_rhs, leaf_inverse, interpolation, skeleton_rows, root_rows, root_rhs, factor,
    leaf_out, root_out,
    inverse_v, factor_v, hot, solved, skel_box, assem, assem_box, vec_send, vec_box,
    acc, stage, box, kept, full, sol_box, take, take_box,
    inverse_sem, factor_sem, skel_send_sem, skel_sem, assem_send_sem, assem_sem,
    vec_send_sem, vec_sem, rs_send_sem, rs_sem, sol_send_sem, sol_sem, take_send_sem, take_sem,
):
    row = lax.axis_index("row")
    col = lax.axis_index("col")
    rhs_here, section = root_rhs.shape
    width = section // cols
    slots = skeleton_rows.shape[1]
    leaf = leaf_rhs.shape[1]

    load_inverse = pltpu.make_async_copy(leaf_inverse, inverse_v, inverse_sem)
    load_inverse.start()
    load_factor = pltpu.make_async_copy(factor, factor_v, factor_sem)

    barrier = pltpu.get_barrier_semaphore()
    for step in range(1, rows):
        pl.semaphore_signal(barrier, inc=1, device_id={"row": lax.rem(row + step, rows)})
    for step in range(1, cols):
        pl.semaphore_signal(barrier, inc=1, device_id={"col": lax.rem(col + step, cols)})

    def build_hot(part, carry):
        start = part * width
        at = lax.broadcasted_iota(jnp.int32, (width, slots), 0) + (start + row * section)
        for leaf_index in range(rows):
            wanted = root_rows[leaf_index:leaf_index + 1, :]
            hot[pl.ds(pl.multiple_of(start, width), width),
                leaf_index * slots:(leaf_index + 1) * slots] = jnp.where(
                    at == wanted, 1.0, 0.0).astype(BF16)
        return carry

    lax.fori_loop(0, cols, build_hot, 0)

    live = lax.broadcasted_iota(jnp.int32, (rhs_here, slots), 1) < ranks[0]

    load_inverse.wait()
    load_factor.start()
    leaf_step = 256
    here = leaf_rhs[...]
    skeleton = jnp.zeros((2 * rhs_here, slots), F32)
    for start in range(0, leaf, leaf_step):
        part = dot_nt(here, inverse_v[start:start + leaf_step, :])
        solved[:, start:start + leaf_step] = part
        at = lax.broadcasted_iota(jnp.int32, (leaf_step, slots), 0) + start
        pick = jnp.where(at == skeleton_rows[...], 1.0, 0.0).astype(BF16)
        skeleton = skeleton + dot_nn(hi_lo(part), pick)
    skeleton = jnp.where(live, skeleton[:rhs_here] + skeleton[rhs_here:], 0.0)
    skel_box[row] = skeleton

    pl.semaphore_wait(barrier, rows + cols - 2)

    def skel_copy(target, source):
        return pltpu.make_async_remote_copy(
            skel_box.at[row], skel_box.at[source], skel_send_sem.at[target],
            skel_sem.at[source], device_id={"row": target})

    for step in range(1, rows):
        target = lax.rem(row + step, rows)
        pltpu.make_async_remote_copy(
            skel_box.at[row], skel_box.at[row], skel_send_sem.at[target],
            skel_sem.at[row], device_id={"row": target}).start()
    for step in range(1, rows):
        source = lax.rem(row + step, rows)
        skel_copy(source, source).wait_recv()

    split = [hi_lo(skel_box[leaf_index]) for leaf_index in range(rows)]
    flat = jnp.concatenate(split, axis=1)

    def assem_copy(target, slot):
        return pltpu.make_async_remote_copy(
            assem.at[target], assem_box.at[slot], assem_send_sem.at[target],
            assem_sem.at[slot], device_id={"col": target})

    def build_assem(step, carry):
        target = lax.rem(col + step, cols)
        start = pl.multiple_of(target * width, width)
        added = dot_nt(flat, hot[pl.ds(start, width), :])
        assem[target] = root_rhs[:, pl.ds(start, width)] + (added[:rhs_here] + added[rhs_here:])

        @pl.when(step < cols)
        def _():
            assem_copy(target, col).start()

        return carry

    lax.fori_loop(1, cols + 1, build_assem, 0)
    assem_box[col] = assem[col]

    def take_assem(step, carry):
        source = lax.rem(col + step, cols)
        assem_copy(source, source).wait_recv()
        return carry

    lax.fori_loop(1, cols, take_assem, 0)
    for source in range(cols):
        kept[source * rhs_here:(source + 1) * rhs_here, :] = assem_box[source]

    load_factor.wait()

    share = rhs_here * cols // GROUPS

    def part_of(group):
        return pl.ds(group * share, share)

    def vec_copy(kind, group, target, slot):
        return pltpu.make_async_remote_copy(
            vec_send.at[kind, part_of(group)], vec_box.at[kind, slot, part_of(group)],
            vec_send_sem.at[kind, target, group], vec_sem.at[kind, slot, group],
            device_id={"row": target})

    def clear():
        def body(part, carry):
            acc[part] = jnp.zeros(acc.shape[1:], F32)
            return carry
        lax.fori_loop(0, cols, body, 0)

    def block(source, part):
        return factor_v[source, pl.ds(pl.multiple_of(part * width, width), width), :]

    def gather_in(kind, group, source):
        vec_copy(kind, group, source, source).wait_recv()

        def body(part, carry):
            acc[part, part_of(group), :] += dot_nt(
                vec_box[kind, source, part_of(group), :], block(source, part))
            return carry

        lax.fori_loop(0, cols, body, 0, unroll=True)

    def rs_copy(phase, group, target, slot):
        return pltpu.make_async_remote_copy(
            stage.at[phase, target, part_of(group)], box.at[phase, slot, part_of(group)],
            rs_send_sem.at[phase, target, group], rs_sem.at[phase, slot, group],
            device_id={"col": target})

    def scatter(phase, group, vector, source, with_acc):
        def send(turn, carry):
            step = cols // 2 + (2 * (turn % 2) - 1) * (turn // 2)
            target = lax.rem(col + step, cols)
            part = dot_nt(vector, block(source, target))
            if with_acc:
                part = part + acc[target, part_of(group), :]
            stage[phase, target, part_of(group), :] = part.astype(BF16)
            rs_copy(phase, group, target, col).start()
            return carry

        lax.fori_loop(1, cols, send, 0, unroll=True)
        total = dot_nt(vector, block(source, col))
        if with_acc:
            total = total + acc[col, part_of(group), :]
        full[part_of(group), :] = total

    def collect(phase, group):
        total = full[part_of(group), :]
        for step in range(1, cols):
            origin = lax.rem(col + cols - step, cols)
            rs_copy(phase, group, origin, origin).wait_recv()
            total = total + box[phase, origin, part_of(group), :].astype(F32)
        return total

    def send_forward(group):
        vec_send[0, part_of(group), :] = kept[part_of(group), :].astype(BF16)
        for step in range(1, rows):
            @pl.when(row + step < rows)
            def _():
                vec_copy(0, group, row + step, row).start()

    @pl.when(row == 0)
    def _():
        for group in range(GROUPS):
            send_forward(group)

    @pl.when(row > 0)
    def _():
        clear()

        def body(source, carry):
            for group in range(GROUPS):
                gather_in(0, group, source)
            return carry

        lax.fori_loop(0, row - 1, body, 0)
        for group in range(GROUPS):
            vec_copy(0, group, row - 1, row - 1).wait_recv()
            scatter(0, group, vec_box[0, row - 1, part_of(group), :], row - 1, True)

        @pl.when(row < rows - 1)
        def _():
            for group in range(GROUPS):
                kept[part_of(group), :] -= collect(0, group)
                send_forward(group)

    @pl.when(row < rows - 1)
    def _():
        clear()

        def body(step, carry):
            for group in range(GROUPS):
                gather_in(1, group, rows - 1 - step)
            return carry

        lax.fori_loop(0, rows - 2 - row, body, 0)
        for group in range(GROUPS):
            vec_copy(1, group, row + 1, row + 1).wait_recv()
            scatter(1, group, vec_box[1, row + 1, part_of(group), :], row + 1, True)

    last = jnp.where(row == rows - 1, 0, 1)
    for group in range(GROUPS):
        low = (kept[part_of(group), :] - collect(last, group)).astype(BF16)
        scatter(2, group, low, row, False)
    for group in range(GROUPS):
        total = collect(2, group)
        full[part_of(group), :] = total
        vec_send[1, part_of(group), :] = total.astype(BF16)
        for step in range(1, rows):
            @pl.when(row - step >= 0)
            def _():
                vec_copy(1, group, row - step, row).start()

    def sol_copy(target, slot):
        return pltpu.make_async_remote_copy(
            full.at[pl.ds(pl.multiple_of(target * rhs_here, rhs_here), rhs_here), :],
            sol_box.at[slot], sol_send_sem.at[target], sol_sem.at[slot],
            device_id={"col": target})

    def send_sol(step, carry):
        sol_copy(lax.rem(col + step, cols), col).start()
        return carry

    lax.fori_loop(1, cols, send_sol, 0)
    sol_box[col] = full[pl.ds(pl.multiple_of(col * rhs_here, rhs_here), rhs_here), :]

    def receive_sol(step, carry):
        origin = lax.rem(col + cols - step, cols)
        sol_copy(origin, origin).wait_recv()
        return carry

    lax.fori_loop(1, cols, receive_sol, 0)
    taken = jnp.zeros((rhs_here, rows * slots), F32)
    for source in range(cols):
        piece = sol_box[source]
        root_out[:, source * width:(source + 1) * width] = piece
        taken = taken + dot_nn(piece.astype(BF16), hot[source * width:(source + 1) * width, :])
    for leaf_index in range(rows):
        take[leaf_index] = taken[:, leaf_index * slots:(leaf_index + 1) * slots]

    def take_copy(target, slot):
        return pltpu.make_async_remote_copy(
            take.at[target], take_box.at[slot], take_send_sem.at[target],
            take_sem.at[slot], device_id={"row": target})

    for step in range(1, rows):
        take_copy(lax.rem(row + step, rows), row).start()
    take_box[row] = take[row]
    for step in range(1, rows):
        source = lax.rem(row + step, rows)
        take_copy(source, source).wait_recv()
    picked = take_box[0]
    for source in range(1, rows):
        picked = picked + take_box[source]
    picked = jnp.where(live, picked, 0.0).astype(BF16)
    leaf_out[...] = solved[...] - dot_nn(picked, interpolation[...])

    for step in range(1, rows):
        target = lax.rem(row + step, rows)
        skel_copy(target, target).wait_send()
        take_copy(target, row).wait_send()

        for group in range(GROUPS):
            @pl.when(row + step < rows)
            def _():
                vec_copy(0, group, row + step, row).wait_send()

            @pl.when(row - step >= 0)
            def _():
                vec_copy(1, group, row - step, row).wait_send()

    def drain(step, carry):
        target = lax.rem(col + step, cols)
        assem_copy(target, col).wait_send()
        sol_copy(target, col).wait_send()
        for group in range(GROUPS):
            rs_copy(2, group, target, col).wait_send()

            @pl.when(row > 0)
            def _():
                rs_copy(0, group, target, col).wait_send()

            @pl.when(row < rows - 1)
            def _():
                rs_copy(1, group, target, col).wait_send()

        return carry

    lax.fori_loop(1, cols, drain, 0)


def on_device(
    rows, cols,
    leaf_rhs, leaf_inverse, interpolation, ranks, skeleton_rows, root_rows, root_rhs, root_factor
):
    _, rhs_here, leaf = leaf_rhs.shape
    slots = skeleton_rows.shape[1]
    section = root_rhs.shape[1]
    width = section // cols
    rhs = rhs_here * cols
    factor = jnp.transpose(root_factor, (1, 0, 2))
    vmem = pl.BlockSpec(memory_space=pltpu.VMEM)
    smem = pl.BlockSpec(memory_space=pltpu.SMEM)
    hbm = pl.BlockSpec(memory_space=pl.ANY)
    dma = pltpu.SemaphoreType.DMA
    leaf_solution, root_solution = pl.pallas_call(
        functools.partial(kernel, rows, cols),
        out_shape=(
            jax.ShapeDtypeStruct((rhs_here, leaf), F32),
            jax.ShapeDtypeStruct((rhs_here, section), F32),
        ),
        in_specs=[smem, vmem, hbm, vmem, vmem, vmem, vmem, hbm],
        out_specs=(vmem, vmem),
        scratch_shapes=[
            pltpu.VMEM((leaf, leaf), BF16),
            pltpu.VMEM((rows, section, width), BF16),
            pltpu.VMEM((section, rows * slots), BF16),
            pltpu.VMEM((rhs_here, leaf), F32),
            pltpu.VMEM((rows, rhs_here, slots), F32),
            pltpu.VMEM((cols, rhs_here, width), F32),
            pltpu.VMEM((cols, rhs_here, width), F32),
            pltpu.VMEM((2, rhs, width), BF16),
            pltpu.VMEM((2, rows, rhs, width), BF16),
            pltpu.VMEM((cols, rhs, width), F32),
            pltpu.VMEM((3, cols, rhs, width), BF16),
            pltpu.VMEM((3, cols, rhs, width), BF16),
            pltpu.VMEM((rhs, width), F32),
            pltpu.VMEM((rhs, width), F32),
            pltpu.VMEM((cols, rhs_here, width), F32),
            pltpu.VMEM((rows, rhs_here, slots), F32),
            pltpu.VMEM((rows, rhs_here, slots), F32),
            dma, dma,
            dma((rows,)), dma((rows,)), dma((cols,)), dma((cols,)),
            dma((2, rows, GROUPS)), dma((2, rows, GROUPS)),
            dma((3, cols, GROUPS)), dma((3, cols, GROUPS)),
            dma((cols,)), dma((cols,)), dma((rows,)), dma((rows,)),
        ],
        compiler_params=pltpu.CompilerParams(
            collective_id=0, has_side_effects=True, vmem_limit_bytes=56 * 1024 * 1024),
        name="root_solve",
    )(
        ranks, leaf_rhs[0], leaf_inverse[0], interpolation[0], skeleton_rows, root_rows,
        root_rhs, factor,
    )
    return leaf_solution[None], root_solution


def solution(mesh):
    in_specs = (
        P("row", "col", None),
        P("row", None, None),
        P("row", None, None),
        P("row"),
        P("row", None),
        P(),
        P("col", "row"),
        P("row", None, "col"),
    )
    out_specs = (P("row", "col", None), P("col", "row"))
    return jax.shard_map(
        functools.partial(on_device, mesh.shape["row"], mesh.shape["col"]),
        mesh=mesh, in_specs=in_specs, out_specs=out_specs, check_vma=False,
    )
```
